1024 devices in a mesh: replica: 32 (over z, y_hi, core), fsdp: 8 (over x), tensor: 4 (over y_lo).
Axes of the slice: x: 8, y: 8 (y_hi: 2, y_lo: 4; y = y_hi * 4 + y_lo), z: 8, core: 2. Of those that a mesh axis runs over, the one named last changes fastest.
Arguments:
- layer_input: bfloat16 [32768, 8192], P(('replica', 'fsdp')), may hold values from -6 to 6
- norm_gain: float32 [8192], replicated, may hold values from 0.5 to 1.5
- value_weight: bfloat16 [32, 8192, 1024], P('replica', 'fsdp', 'tensor'), may hold values from -0.0625 to 0.0625
- value_cotangent: bfloat16 [32768, 1024], P(('replica', 'fsdp'), 'tensor'), may hold values from -3 to 3
- token_ids: int32 [32768], P(('replica', 'fsdp')), may hold values from 0 to 128255, as said below
- anchor_weight: float32 [32, 2048, 1024], P('replica', 'fsdp', 'tensor'), may hold values from -0.0625 to 0.0625
- outer_momentum: float32 [32, 2048, 1024], P('replica', 'fsdp', 'tensor'), may hold values from -0.0625 to 0.0625
- gossip_exponent: int32 [4], replicated, may hold values from 0 to 4
- fragment_index: int32 [1], replicated, may hold values from 0 to 3
Outputs:
- value: bfloat16 [32768, 1024], P(('replica', 'fsdp'), 'tensor')
- input_grad: bfloat16 [32768, 8192], P(('replica', 'fsdp'), 'tensor')
- weight_grad: bfloat16 [32, 8192, 1024], P('replica', 'fsdp', 'tensor')
- new_anchor: float32 [32, 2048, 1024], P('replica', 'fsdp', 'tensor')
- new_momentum: float32 [32, 2048, 1024], P('replica', 'fsdp', 'tensor')
- merged_weight: bfloat16 [32, 2048, 1024], P('replica', 'fsdp', 'tensor')
The draws below stay inside these ranges and needn't reach their ends.
Inputs may be any that keep to these rules, and one draw needn't show every extreme that they name: `token_ids`: some of the ids are the padding id 128004.
All inputs are finite; a program needn't handle non-finite values.
Results may differ from the reference program's by a relative error of at most 0.019.
Values may be sent and summed in bfloat16 or wider, within the bound.
A program may use at most 64 MiB of HBM per device.

```python
import jax
import jax.numpy as jnp
from jax import lax

D = 8192
KVW = 1024
VOCAB = 128256
TOK_DEV = 128
NFRAG = 4
FRAG_ROWS = 256
TOKENS = 32768
FRAG_D = 2048
REPL_BITS = 5
N_REPLICA = 32
N_FSDP = 8
N_TENSOR = 4


def draw_token_ids(key, part):
    key = jax.random.fold_in(key, 11)
    first, second = jax.random.split(key)
    ids = jax.random.randint(first, (TOKENS,), 0, VOCAB, dtype=jnp.int32)
    padded = jax.random.randint(second, (TOKENS,), 0, 8, dtype=jnp.int32) == 0
    return jnp.where(padded, jnp.int32(128004), ids)


def place_ends(array, own_key, least, top_value):
    longest = array.shape.index(max(array.shape))
    spots = []
    for shift in (0, 1):
        where = [jax.random.randint(jax.random.fold_in(own_key, axis), (), 0, length) for axis, length in enumerate(array.shape)]
        where[longest] = (where[longest] + shift) % array.shape[longest]
        spots.append(tuple(where))
    return array.at[spots[0]].set(least).at[spots[1]].set(top_value)


def block_levels(own_key, extent, shards, least, top_value):
    level, own = 1.0, jax.random.fold_in(own_key, 6)
    for position, shards_of in shards:
        heights = jnp.exp(jax.random.uniform(jax.random.fold_in(own, position), (shards_of,), jnp.float32, least / len(shards), top_value / len(shards)))
        level = level * jnp.repeat(heights, extent[position] // shards_of).reshape([-1 if axis == position else 1 for axis in range(len(extent))])
    return level


def centred(own_key, dims, scale, reach, shards=(), kind=jnp.bfloat16):
    result = scale * jax.random.normal(own_key, dims, jnp.float32)
    if shards:
        result = result * block_levels(own_key, dims, shards, -0.22, 0.18)
    return jnp.clip(result, -reach, reach).astype(kind)


def setup_inputs(seed: int = 0) -> dict:
    keys = jax.random.split(jax.random.key(seed), 10)
    layer_input = centred(keys[0], (TOKENS, D), 1.0, 6.0, ((0, 256),))
    norm_gain = jnp.clip(1.0 + 0.1 * jax.random.normal(keys[1], (D,), jnp.float32), 0.5, 1.5)
    value_weight = centred(keys[2], (N_REPLICA, D, KVW), D ** -0.5, 0.0625, ((0, 32), (1, 8), (2, 4)))
    value_cotangent = centred(keys[3], (TOKENS, KVW), 0.5, 3.0, ((0, 256), (1, 4)))
    token_ids = draw_token_ids(jax.random.fold_in(keys[9], 71), 0)
    anchor_weight = centred(keys[5], (N_REPLICA, FRAG_D, KVW), D ** -0.5, 0.0625, ((0, 32), (1, 8), (2, 4)), jnp.float32)
    outer_momentum = centred(keys[6], (N_REPLICA, FRAG_D, KVW), D ** -0.5, 0.0625, ((0, 32), (1, 8), (2, 4)), jnp.float32)
    gossip_exponent = place_ends(jax.random.randint(keys[7], (NFRAG,), 0, REPL_BITS), jax.random.fold_in(keys[7], 1), 0, REPL_BITS - 1).astype(jnp.int32)
    fragment_index = jax.random.randint(keys[8], (1,), 0, NFRAG).astype(jnp.int32)
    return dict(layer_input=layer_input, norm_gain=norm_gain, value_weight=value_weight, value_cotangent=value_cotangent, token_ids=token_ids, anchor_weight=anchor_weight, outer_momentum=outer_momentum, gossip_exponent=gossip_exponent, fragment_index=fragment_index)


pad_token = 128004
outer_mu = 0.9
outer_eta = 0.7
merge_alpha = 0.5

def replica_layer(args, norm_gain):
    inputs, ids, cotan_in, weight = args
    xf = inputs.astype(jnp.float32)
    inv = lax.rsqrt(lax.optimization_barrier(jnp.mean(xf * xf, axis=1)) + 1e-05)
    normed = (xf * inv[:, None] * norm_gain[None, :]).astype(jnp.bfloat16)
    value = jnp.dot(normed, weight, preferred_element_type=jnp.float32).astype(jnp.bfloat16)
    keep = (ids != pad_token).astype(jnp.bfloat16)
    cotan = cotan_in * keep[:, None]
    grad = jnp.dot(normed.T, cotan, preferred_element_type=jnp.float32).astype(jnp.bfloat16)
    width = KVW // N_TENSOR
    back = jnp.zeros(xf.shape, jnp.float32)
    for block in range(N_TENSOR):
        part = jnp.dot(cotan[:, block * width:(block + 1) * width], weight[:, block * width:(block + 1) * width].T, preferred_element_type=jnp.float32).astype(jnp.bfloat16)
        part = lax.optimization_barrier(part)
        back = back + part.astype(jnp.float32)
    return (value, back.astype(jnp.bfloat16), grad)

def reference(layer_input, norm_gain, value_weight, value_cotangent, token_ids, anchor_weight, outer_momentum, gossip_exponent, fragment_index):
    rows_rep = TOK_DEV * N_FSDP
    inputs = layer_input.reshape(N_REPLICA, rows_rep, D)
    ids = token_ids.reshape(N_REPLICA, rows_rep)
    cotan = value_cotangent.reshape(N_REPLICA, rows_rep, KVW)
    value, dinput, grad = lax.map(lambda a: replica_layer(a, norm_gain), (inputs, ids, cotan, value_weight))
    value = value.reshape(TOKENS, KVW)
    dinput = dinput.reshape(TOKENS, D)
    blocks = D // (NFRAG * FRAG_ROWS)
    shape5 = (N_REPLICA, blocks, NFRAG, FRAG_ROWS, KVW)
    index = fragment_index[0]
    weight_f = lax.dynamic_index_in_dim(value_weight.astype(jnp.float32).reshape(shape5), index, 2, keepdims=False)
    weight_f = weight_f.reshape(N_REPLICA, FRAG_D, KVW)
    own = anchor_weight - weight_f
    expo = lax.dynamic_index_in_dim(gossip_exponent, index, 0, keepdims=False)
    partner = jnp.bitwise_xor(jnp.arange(N_REPLICA, dtype=jnp.int32), jnp.left_shift(jnp.int32(1), expo))
    mean_delta = 0.5 * (own + own[partner])
    momentum_new = outer_mu * outer_momentum + mean_delta
    anchor_new = anchor_weight - outer_eta * (mean_delta + outer_mu * momentum_new)
    merged = (merge_alpha * weight_f + (1.0 - merge_alpha) * anchor_new).astype(jnp.bfloat16)
    return (value, dinput, grad, anchor_new, momentum_new, merged)
```

```python
import functools

import jax
import jax.numpy as jnp
from jax import lax
from jax.experimental import pallas as pl
from jax.experimental.pallas import tpu as pltpu
from jax.sharding import PartitionSpec as P

MESH = pl.DeviceIdType.MESH
PAD = 128004
MU = 0.9
ETA = 0.7
ALPHA = 0.5
NX = 8
NY = 4
BITS = 5
TOK = 128
DF = 1024
HALF = 512
KV = 256
ORDER = (1, 7, 2, 6, 3, 5, 4)


def contract(left, right, dims):
    return lax.dot_general(left, right, (dims, ((), ())), preferred_element_type=jnp.float32)


def kernel(
    plan_ref, frag_ref, ids_ref, x_ref, gain_ref, w_ref, c_ref, anchor_ref, mom_ref,
    value_ref, back_ref, grad_ref, new_anchor_ref, new_mom_ref, merged_ref,
    c_all, xn, xr, part, got, fin, vsend, vr, delta, gossip, inv_ref,
    c_send, c_recv, x_send, x_recv, h_send, h_recv, v_send, v_recv,
    p_send, p_recv, b_send, b_recv, g_send, g_recv,
):
    r = lax.axis_index("replica")
    f = lax.axis_index("fsdp")
    t = lax.axis_index("tensor")
    h = lax.rem(t, 2)
    mate = t + 1 - 2 * h

    def column(offset):
        return lax.rem(f + offset + NX, NX)

    def row(offset):
        return lax.rem(t + offset, NY)

    def partner(bit):
        own = lax.rem(r // (1 << bit), 2)
        return r + (1 << bit) * (1 - 2 * own)

    def push(src, dst, send, recv, **where):
        return pltpu.make_async_remote_copy(
            src_ref=src, dst_ref=dst, send_sem=send, recv_sem=recv, device_id=where, device_id_type=MESH
        )

    home = f // 2
    side = lax.rem(f, 2)
    slots = (t, t + NY)
    homes = [column(-slot) for slot in slots]
    stays = jnp.logical_and(t == 0, home == 0)

    barrier = pltpu.get_barrier_semaphore()

    def greet(**where):
        pl.semaphore_signal(barrier, inc=1, device_id=where, device_id_type=MESH)

    for d in range(1, NX):
        greet(fsdp=column(d))
    for s in range(1, NY):
        greet(tensor=row(s))
    for bit in range(BITS):
        greet(replica=partner(bit))
    for j in range(2):
        origin = 2 * t + j
        gap = lax.rem(origin - f + NX, NX)

        @pl.when(jnp.logical_not(jnp.logical_and(gap == 0, t == 0)))
        def _():
            greet(fsdp=origin, tensor=lax.rem(gap, NY))

    keep = jnp.where(ids_ref[...] != PAD, 1.0, 0.0).astype(jnp.float32)
    keep = jnp.broadcast_to(keep, (TOK, TOK)).T
    for j in range(KV // TOK):
        cols = slice(j * TOK, (j + 1) * TOK)
        c_all[0, :, cols] = (c_ref[:, cols].astype(jnp.float32) * keep).astype(jnp.bfloat16)
    p = frag_ref[0]
    expo = plan_ref[p]
    own_delta = anchor_ref[...] - w_ref[p].astype(jnp.float32)
    delta[...] = own_delta.astype(jnp.bfloat16)

    pl.semaphore_wait(barrier, NX - 1 + NY - 1 + BITS + 2 - jnp.where(stays, 1, 0))

    c_copies = {
        d: push(c_all.at[0], c_all.at[d], c_send.at[d], c_recv.at[d], fsdp=column(d)) for d in ORDER
    }
    for d in ORDER:
        c_copies[d].start()
    g_copies = [
        push(delta, gossip.at[bit], g_send.at[bit], g_recv.at[bit], replica=partner(bit)) for bit in range(BITS)
    ]
    for copy in g_copies:
        copy.start()

    def squares(i, acc):
        start = pl.multiple_of(i * DF, DF)
        block = x_ref[:, pl.ds(start, DF)].astype(jnp.float32)
        for j in range(DF // 128):
            piece = block[:, j * 128 : (j + 1) * 128]
            acc = acc + piece * piece
        return acc

    acc = lax.fori_loop(0, NX, squares, jnp.zeros((TOK, 128), jnp.float32))
    mean = jnp.sum(acc, axis=1, keepdims=True) * (1.0 / (NX * DF))
    inv_ref[...] = jnp.broadcast_to(lax.rsqrt(mean + 1e-05), (TOK, 128))

    def normed(start, width):
        start = pl.multiple_of(start, HALF)
        block = x_ref[:, pl.ds(start, width)].astype(jnp.float32)
        return (block * inv_ref[:, :1] * gain_ref[:, pl.ds(start, width)]).astype(jnp.bfloat16)

    x_copies = {}
    for d in ORDER:
        there = column(d)
        xn[d] = normed(there * DF + h * HALF, HALF)
        x_copies[d] = push(xn.at[d], xr.at[h, d], x_send.at[d], x_recv.at[d], fsdp=there)
        x_copies[d].start()
    for side_h in range(2):
        xr[side_h, 0] = normed(f * DF + side_h * HALF, HALF)

    for d in ORDER:
        c_copies[d].wait_recv()
    weight = w_ref[...].reshape(DF, KV)
    p_copies = []
    for s in (2, 1, 3, 0):
        for j in range(2):
            slot = row(s) + j * NY
            part[s, j] = contract(c_all[slot], weight, ((1,), (1,))).astype(jnp.bfloat16)
        if s:
            copy = push(part.at[s], got.at[s], p_send.at[s], p_recv.at[s], tensor=row(s))
            copy.start()
            p_copies.append(copy)

    def values(d):
        lo = contract(xr[0, d], weight[:HALF], ((1,), (0,)))
        hi = contract(xr[1, d], weight[HALF:], ((1,), (0,)))
        return lo + hi

    h_copies = {}
    for d in ORDER:
        x_copies[d].wait_recv()
        h_copies[d] = push(xr.at[h, d], xr.at[h, d], h_send.at[d], h_recv.at[d], tensor=mate)
        h_copies[d].start()
    v_copies = {}
    for d in ORDER:
        h_copies[d].wait_recv()
        vsend[d] = values(d).astype(jnp.bfloat16)
        v_copies[d] = push(vsend.at[d], vr.at[d], v_send.at[d], v_recv.at[d], fsdp=column(-d))
        v_copies[d].start()

    for copy in g_copies:
        copy.wait_recv()
    own_weight = w_ref[p].astype(jnp.float32)
    anchor = anchor_ref[...]
    mean_delta = 0.5 * (anchor - own_weight + gossip[expo].astype(jnp.float32))
    momentum = MU * mom_ref[...] + mean_delta
    new_anchor = anchor - ETA * (mean_delta + MU * momentum)
    new_mom_ref[...] = momentum
    new_anchor_ref[...] = new_anchor
    merged_ref[...] = (ALPHA * own_weight + (1.0 - ALPHA) * new_anchor).astype(jnp.bfloat16)

    for copy in p_copies:
        copy.wait_recv()
    for j in range(2):
        total = part[0, j].astype(jnp.float32)
        for s in range(1, NY):
            total = total + got[s, j].astype(jnp.float32)
        fin[j] = total.astype(jnp.bfloat16)
    place = back_ref.at[:, pl.ds(pl.multiple_of(side * DF, DF), DF)]
    b_copies = [
        push(fin.at[j], place, b_send.at[j], b_recv.at[side], fsdp=homes[j], tensor=home) for j in range(2)
    ]
    kept = pltpu.make_async_copy(fin.at[0], place, b_recv.at[side])

    @pl.when(stays)
    def _():
        kept.start()

    @pl.when(jnp.logical_not(stays))
    def _():
        b_copies[0].start()

    b_copies[1].start()

    cotan = c_all[...].reshape(NX * TOK, KV)
    for side_h in range(2):
        block = contract(cotan, xr[side_h].reshape(NX * TOK, HALF), ((0,), (0,)))
        grad_ref[side_h * HALF : (side_h + 1) * HALF, :] = block.T.astype(jnp.bfloat16)

    total = values(0)
    for d in ORDER:
        v_copies[d].wait_recv()
        total = total + vr[d].astype(jnp.float32)
    value_ref[...] = total.astype(jnp.bfloat16)

    for j in range(2):
        pltpu.make_async_copy(fin.at[j], back_ref.at[:, j * DF : (j + 1) * DF], b_recv.at[j]).wait()

    @pl.when(jnp.logical_not(stays))
    def _():
        b_copies[0].wait_send()

    b_copies[1].wait_send()
    for d in ORDER:
        c_copies[d].wait_send()
        x_copies[d].wait_send()
        h_copies[d].wait_send()
        v_copies[d].wait_send()
    for copy in p_copies + g_copies:
        copy.wait_send()


def local(
    layer_input, norm_gain, value_weight, value_cotangent, token_ids,
    anchor_weight, outer_momentum, gossip_exponent, fragment_index,
):
    bf16, f32 = jnp.bfloat16, jnp.float32
    smem = pl.BlockSpec(memory_space=pltpu.SMEM)
    vmem = pl.BlockSpec(memory_space=pltpu.VMEM)
    dma = pltpu.SemaphoreType.DMA
    frag = anchor_weight.shape[1:]
    outs = pl.pallas_call(
        kernel,
        out_shape=(
            jax.ShapeDtypeStruct((TOK, KV), bf16),
            jax.ShapeDtypeStruct((TOK, 2 * DF), bf16),
            jax.ShapeDtypeStruct((DF, KV), bf16),
            jax.ShapeDtypeStruct(frag, f32),
            jax.ShapeDtypeStruct(frag, f32),
            jax.ShapeDtypeStruct(frag, bf16),
        ),
        in_specs=[smem, smem] + [vmem] * 7,
        out_specs=[vmem] * 6,
        scratch_shapes=[
            pltpu.VMEM((NX, TOK, KV), bf16),
            pltpu.VMEM((NX, TOK, HALF), bf16),
            pltpu.VMEM((2, NX, TOK, HALF), bf16),
            pltpu.VMEM((NY, 2, TOK, DF), bf16),
            pltpu.VMEM((NY, 2, TOK, DF), bf16),
            pltpu.VMEM((2, TOK, DF), bf16),
            pltpu.VMEM((NX, TOK, KV), bf16),
            pltpu.VMEM((NX, TOK, KV), bf16),
            pltpu.VMEM(frag, bf16),
            pltpu.VMEM((BITS, *frag), bf16),
            pltpu.VMEM((TOK, 128), f32),
            dma((NX,)), dma((NX,)), dma((NX,)), dma((NX,)), dma((NX,)), dma((NX,)), dma((NX,)), dma((NX,)),
            dma((NY,)), dma((NY,)), dma((2,)), dma((2,)), dma((BITS,)), dma((BITS,)),
        ],
        compiler_params=pltpu.CompilerParams(
            collective_id=0, has_side_effects=True, vmem_limit_bytes=48 * 1024 * 1024
        ),
        cost_estimate=pl.CostEstimate(flops=2 * 10**9, bytes_accessed=6 * 10**6, transcendentals=128),
    )(
        gossip_exponent, fragment_index, token_ids.reshape(1, TOK), layer_input, norm_gain.reshape(1, NX * DF),
        value_weight.reshape(4, KV, KV), value_cotangent, anchor_weight[0], outer_momentum[0],
    )
    value, back, grad, new_anchor, new_momentum, merged = outs
    return value, back, grad[None], new_anchor[None], new_momentum[None], merged[None]


def solution(mesh):
    tokens = ("replica", "fsdp")
    whole = P("replica", "fsdp", "tensor")
    return jax.shard_map(
        local,
        mesh=mesh,
        in_specs=(P(tokens, None), P(), whole, P(tokens, "tensor"), P(tokens), whole, whole, P(), P()),
        out_specs=(P(tokens, "tensor"), P(tokens, "tensor"), whole, whole, whole, whole),
        check_vma=False,
    )
```

```python
import functools

import jax
import jax.numpy as jnp
from jax import lax
from jax.experimental import pallas as pl
from jax.experimental.pallas import tpu as pltpu
from jax.sharding import PartitionSpec as P

MESH = pl.DeviceIdType.MESH
PAD = 128004
MU = 0.9
ETA = 0.7
ALPHA = 0.5
NX = 8
NY = 4
BITS = 5
TOK = 128
DF = 1024
HALF = 512
KV = 256
ORDER = (1, 7, 2, 6, 3, 5, 4)


def contract(left, right, dims):
    return lax.dot_general(left, right, (dims, ((), ())), preferred_element_type=jnp.float32)


def kernel(
    plan_ref, frag_ref, ids_hbm, x_hbm, gain_hbm, w_hbm, c_hbm, anchor_hbm, mom_hbm,
    value_ref, back_ref, grad_ref, new_anchor_ref, new_mom_ref, merged_ref,
    ids_ref, x_ref, gain_ref, w_ref, c_ref, anchor_ref, mom_ref,
    c_all, c_four, w_all, xn, xr, fin, vsend, vr, delta, gossip, inv_ref,
    load, c_send, c_recv, cy_send, cy_recv, four_send, four_recv, w_send, w_recv,
    x_send, near_send, near_recv, far_send, far_recv, v_send, v_recv, b_send, b_recv, g_send, g_recv,
):
    r = lax.axis_index("replica")
    f = lax.axis_index("fsdp")
    t = lax.axis_index("tensor")
    h = t // 2
    inward = t + 1 - 2 * h
    outward = t - 1 + 2 * h
    middle = jnp.logical_or(t == 1, t == 2)
    end = jnp.logical_not(middle)

    def column(offset):
        return lax.rem(f + offset + NX, NX)

    def partner(bit):
        own = lax.rem(r // (1 << bit), 2)
        return r + (1 << bit) * (1 - 2 * own)

    def push(src, dst, send, recv, **where):
        return pltpu.make_async_remote_copy(
            src_ref=src, dst_ref=dst, send_sem=send, recv_sem=recv, device_id=where, device_id_type=MESH
        )

    w_own = w_all.at[t]
    pairs = (
        (c_hbm, c_ref), (ids_hbm, ids_ref), (w_hbm, w_own), (x_hbm, x_ref), (gain_hbm, gain_ref),
        (anchor_hbm, anchor_ref), (mom_hbm, mom_ref), (w_hbm, w_ref),
    )
    loads = [pltpu.make_async_copy(src, dst, load.at[i]) for i, (src, dst) in enumerate(pairs)]
    for copy in loads:
        copy.start()

    home = f // 2
    side = lax.rem(f, 2)
    stays = jnp.logical_and(t == 1, home == 1)

    barrier = pltpu.get_barrier_semaphore()

    def greet(**where):
        pl.semaphore_signal(barrier, inc=1, device_id=where, device_id_type=MESH)

    greet(tensor=inward)
    for d in range(1, NX):
        greet(fsdp=column(d))
    for bit in range(BITS):
        greet(replica=partner(bit))

    @pl.when(middle)
    def _():
        greet(tensor=outward)
        greet(tensor=3 * (1 - h))

    for j in range(2):
        origin = 2 * t + j
        gap = lax.rem(origin - f + NX, NX)

        @pl.when(jnp.logical_not(jnp.logical_and(gap == 0, t == 1)))
        def _():
            greet(fsdp=origin, tensor=1 + lax.rem(gap, 2))

    loads[0].wait()
    loads[1].wait()
    keep = jnp.where(ids_ref[...] != PAD, 1.0, 0.0).astype(jnp.float32)
    keep = jnp.broadcast_to(keep, (TOK, TOK)).T
    for j in range(KV // TOK):
        cols = slice(j * TOK, (j + 1) * TOK)
        c_all[0, :, cols] = (c_ref[:, cols].astype(jnp.float32) * keep).astype(jnp.bfloat16)
    loads[2].wait()

    pl.semaphore_wait(barrier, NX - 1 + BITS + 2 + jnp.where(middle, 4, 0) - jnp.where(stays, 1, 0))

    c_copies = {d: push(c_all.at[0], c_all.at[d], c_send.at[d], c_recv.at[d], fsdp=column(d)) for d in ORDER}
    cy_in = push(c_all.at[0], c_four.at[NY, t], cy_send.at[0], cy_recv.at[t], tensor=inward)
    cy_over = push(c_all.at[0], c_four.at[NY, t], cy_send.at[1], cy_recv.at[t], tensor=2 - h)
    four = [
        push(c_four.at[NY], c_four.at[i], four_send.at[i], four_recv.at[i], fsdp=column(d))
        for i, d in enumerate((0, 2, 4, 6))
    ]
    four_odd = [
        push(c_four.at[NY], c_four.at[i], four_send.at[i], four_recv.at[i], fsdp=column(d))
        for i, d in enumerate((1, 3, 5, 7))
    ]
    w_in = push(w_own, w_own, w_send.at[0], w_recv.at[t], tensor=inward)
    w_pass = push(w_all.at[outward], w_all.at[outward], w_send.at[1], w_recv.at[outward], tensor=inward)
    near_in = {d: push(xr.at[h, d], xr.at[h, d], near_send.at[d], near_recv.at[d], tensor=inward) for d in ORDER}
    near_across = {d: push(xr.at[h, d], xr.at[h, d], near_send.at[d], far_recv.at[d], tensor=inward) for d in ORDER}
    far_out = {
        d: push(xr.at[1 - h, d], xr.at[1 - h, d], far_send.at[d], far_recv.at[d], tensor=outward) for d in ORDER
    }
    x_copies = {d: push(xn.at[d], xr.at[h, d], x_send.at[d], near_recv.at[d], fsdp=column(d)) for d in ORDER}
    v_copies = {d: push(vsend.at[d], vr.at[d], v_send.at[d], v_recv.at[d], fsdp=column(-d)) for d in ORDER}
    g_copies = [
        push(delta, gossip.at[bit], g_send.at[bit], g_recv.at[bit], replica=partner(bit)) for bit in range(BITS)
    ]
    place = back_ref.at[:, pl.ds(pl.multiple_of(side * DF, DF), DF)]

    def norm_scale():
        def squares(i, acc):
            start = pl.multiple_of(i * DF, DF)
            block = x_ref[:, pl.ds(start, DF)].astype(jnp.float32)
            for j in range(DF // 128):
                piece = block[:, j * 128 : (j + 1) * 128]
                acc = acc + piece * piece
            return acc

        loads[3].wait()
        loads[4].wait()
        acc = lax.fori_loop(0, NX, squares, jnp.zeros((TOK, 128), jnp.float32))
        mean = jnp.sum(acc, axis=1, keepdims=True) * (1.0 / (NX * DF))
        inv_ref[...] = jnp.broadcast_to(lax.rsqrt(mean + 1e-05), (TOK, 128))

    def normed(start):
        start = pl.multiple_of(start, HALF)
        block = x_ref[:, pl.ds(start, HALF)].astype(jnp.float32)
        return (block * inv_ref[:, :1] * gain_ref[:, pl.ds(start, HALF)]).astype(jnp.bfloat16)

    def own_tokens():
        for j in range(2):
            xr[j, 0] = normed(f * DF + j * HALF)

    p = frag_ref[0]

    def send_delta():
        loads[5].wait()
        loads[6].wait()
        loads[7].wait()
        delta[...] = (anchor_ref[...] - w_ref[p].astype(jnp.float32)).astype(jnp.bfloat16)
        for copy in g_copies:
            copy.start()

    def values(d):
        weight = w_ref[...].reshape(DF, KV)
        lo = contract(xr[0, d], weight[:HALF], ((1,), (0,)))
        hi = contract(xr[1, d], weight[HALF:], ((1,), (0,)))
        return lo + hi

    def send_values(d):
        vsend[d] = values(d).astype(jnp.bfloat16)
        v_copies[d].start()

    @pl.when(end)
    def _():
        w_in.start()
        cy_in.start()
        cy_over.start()
        for d in ORDER:
            c_copies[d].start()
        norm_scale()
        for d in ORDER:
            xn[d] = normed(column(d) * DF + h * HALF)
            x_copies[d].start()
        own_tokens()
        send_delta()
        for d in ORDER:
            x_copies[d].wait_recv()
            near_in[d].start()
        for d in ORDER:
            far_out[d].wait_recv()
            send_values(d)
        for d in ORDER:
            c_copies[d].wait_recv()

    def middle_row(row):
        parity = row - 1
        slots = [d for d in (0, *ORDER) if d % 2 == parity]
        others = [d for d in ORDER if d % 2 != parity]
        fours = dict(zip((parity, parity + 2, parity + 4, parity + 6), (four_odd if parity else four)))
        back = {
            d: push(fin.at[d // 2], place, b_send.at[d // 2], b_recv.at[side], fsdp=column(-d), tensor=home)
            for d in slots
        }
        kept = pltpu.make_async_copy(fin.at[0], place, b_recv.at[side])

        def finish(d):
            if d:
                fours[d].wait_recv()
                c_all[d] = c_four[d // 2, row]
            held = d // 2 if d else NY
            total = jnp.zeros((TOK, DF), jnp.float32)
            for block in range(NY):
                total = total + contract(c_four[held, block], w_all[block].reshape(DF, KV), ((1,), (1,)))
            fin[d // 2] = total.astype(jnp.bfloat16)
            if d:
                back[d].start()
            else:

                @pl.when(stays)
                def _():
                    kept.start()

                @pl.when(jnp.logical_not(stays))
                def _():
                    back[0].start()

        cy_in.start()
        w_in.start()
        c_four[NY, row] = c_all[0]
        for block in range(NY):
            if block != row:
                push(c_all.at[0], c_four.at[NY, block], cy_send.at[0], cy_recv.at[block], tensor=inward).wait_recv()
        for d in slots:
            if d:
                fours[d].start()
        for d in others:
            c_copies[d].start()
        norm_scale()
        own_tokens()
        send_delta()
        push(w_own, w_all.at[outward], w_send.at[0], w_recv.at[outward], tensor=inward).wait_recv()
        w_pass.start()
        lag = 2
        for step in range(len(ORDER) + lag):
            if step < len(ORDER):
                near_in[ORDER[step]].wait_recv()
                near_across[ORDER[step]].start()
            if step == 3:
                push(w_own, w_all.at[inward], w_send.at[0], w_recv.at[inward], tensor=inward).wait_recv()
                past = 3 * (1 - h)
                push(w_own, w_all.at[past], w_send.at[0], w_recv.at[past], tensor=inward).wait_recv()
            if 3 <= step < 7:
                finish(slots[step - 3])
            if step >= lag:
                d = ORDER[step - lag]
                far_out[d].wait_recv()
                far_out[d].start()
                send_values(d)
        for d in others:
            c_copies[d].wait_recv()
        for d in others:
            c_copies[d].wait_send()
        for d in slots:
            if d:
                fours[d].wait_send()
                back[d].wait_send()
        if 0 in slots:

            @pl.when(jnp.logical_not(stays))
            def _():
                back[0].wait_send()

    for row in (1, 2):
        pl.when(t == row)(functools.partial(middle_row, row))

    for copy in g_copies:
        copy.wait_recv()
    expo = plan_ref[p]
    own_weight = w_ref[p].astype(jnp.float32)
    anchor = anchor_ref[...]
    mean_delta = 0.5 * (anchor - own_weight + gossip[expo].astype(jnp.float32))
    momentum = MU * mom_ref[...] + mean_delta
    new_anchor = anchor - ETA * (mean_delta + MU * momentum)
    new_mom_ref[...] = momentum
    new_anchor_ref[...] = new_anchor
    merged_ref[...] = (ALPHA * own_weight + (1.0 - ALPHA) * new_anchor).astype(jnp.bfloat16)

    cotan = c_all[...].reshape(NX * TOK, KV)
    for j in range(2):
        block = contract(cotan, xr[j].reshape(NX * TOK, HALF), ((0,), (0,)))
        grad_ref[j * HALF : (j + 1) * HALF, :] = block.T.astype(jnp.bfloat16)

    total = values(0)
    for d in ORDER:
        v_copies[d].wait_recv()
        total = total + vr[d].astype(jnp.float32)
    value_ref[...] = total.astype(jnp.bfloat16)

    for j in range(2):
        pltpu.make_async_copy(fin.at[j], back_ref.at[:, j * DF : (j + 1) * DF], b_recv.at[j]).wait()

    w_in.wait_send()
    cy_in.wait_send()
    for d in ORDER:
        near_in[d].wait_send()
        v_copies[d].wait_send()
    for copy in g_copies:
        copy.wait_send()

    @pl.when(end)
    def _():
        cy_over.wait_send()
        for d in ORDER:
            c_copies[d].wait_send()
            x_copies[d].wait_send()

    @pl.when(middle)
    def _():
        w_pass.wait_send()
        for d in ORDER:
            far_out[d].wait_send()


def write_out(*refs):
    n = len(refs) // 2
    copies = [pltpu.make_async_copy(refs[i], refs[n + i], refs[-1].at[i]) for i in range(n)]
    for copy in copies:
        copy.start()
    for copy in copies:
        copy.wait()


def local(
    layer_input, norm_gain, value_weight, value_cotangent, token_ids,
    anchor_weight, outer_momentum, gossip_exponent, fragment_index,
):
    bf16, f32 = jnp.bfloat16, jnp.float32
    smem = pl.BlockSpec(memory_space=pltpu.SMEM)
    vmem = pl.BlockSpec(memory_space=pltpu.VMEM)
    anywhere = pl.BlockSpec(memory_space=pl.ANY)
    dma = pltpu.SemaphoreType.DMA
    frag = anchor_weight.shape[1:]
    shapes = (
        jax.ShapeDtypeStruct((TOK, KV), bf16),
        jax.ShapeDtypeStruct((TOK, 2 * DF), bf16),
        jax.ShapeDtypeStruct((DF, KV), bf16),
        jax.ShapeDtypeStruct(frag, f32),
        jax.ShapeDtypeStruct(frag, f32),
        jax.ShapeDtypeStruct(frag, bf16),
    )
    outs = pl.pallas_call(
        kernel,
        out_shape=shapes,
        in_specs=[smem, smem] + [anywhere] * 7,
        out_specs=[vmem] * 6,
        scratch_shapes=[
            pltpu.VMEM((1, TOK), jnp.int32),
            pltpu.VMEM((TOK, NX * DF), bf16),
            pltpu.VMEM((1, NX * DF), f32),
            pltpu.VMEM((4, KV, KV), bf16),
            pltpu.VMEM((TOK, KV), bf16),
            pltpu.VMEM(frag, f32),
            pltpu.VMEM(frag, f32),
            pltpu.VMEM((NX, TOK, KV), bf16),
            pltpu.VMEM((NY + 1, NY, TOK, KV), bf16),
            pltpu.VMEM((NY, 4, KV, KV), bf16),
            pltpu.VMEM((NX, TOK, HALF), bf16),
            pltpu.VMEM((2, NX, TOK, HALF), bf16),
            pltpu.VMEM((4, TOK, DF), bf16),
            pltpu.VMEM((NX, TOK, KV), bf16),
            pltpu.VMEM((NX, TOK, KV), bf16),
            pltpu.VMEM(frag, bf16),
            pltpu.VMEM((BITS, *frag), bf16),
            pltpu.VMEM((TOK, 128), f32),
            dma((8,)), dma((NX,)), dma((NX,)), dma((2,)), dma((NY,)), dma((4,)), dma((4,)), dma((2,)), dma((NY,)),
            dma((NX,)), dma((NX,)), dma((NX,)), dma((NX,)), dma((NX,)),
            dma((NX,)), dma((NX,)), dma((4,)), dma((2,)), dma((BITS,)), dma((BITS,)),
        ],
        compiler_params=pltpu.CompilerParams(
            collective_id=0, has_side_effects=True, vmem_limit_bytes=56 * 1024 * 1024
        ),
        cost_estimate=pl.CostEstimate(flops=2 * 10**9, bytes_accessed=6 * 10**6, transcendentals=128),
    )(
        gossip_exponent, fragment_index, token_ids.reshape(1, TOK), layer_input, norm_gain.reshape(1, NX * DF),
        value_weight.reshape(4, KV, KV), value_cotangent, anchor_weight[0], outer_momentum[0],
    )
    outs = pl.pallas_call(
        write_out,
        out_shape=shapes,
        in_specs=[vmem] * 6,
        out_specs=[anywhere] * 6,
        scratch_shapes=[dma((6,))],
    )(*outs)
    value, back, grad, new_anchor, new_momentum, merged = outs
    return value, back, grad[None], new_anchor[None], new_momentum[None], merged[None]


def solution(mesh):
    tokens = ("replica", "fsdp")
    whole = P("replica", "fsdp", "tensor")
    return jax.shard_map(
        local,
        mesh=mesh,
        in_specs=(P(tokens, None), P(), whole, P(tokens, "tensor"), P(tokens), whole, whole, P(), P()),
        out_specs=(P(tokens, "tensor"), P(tokens, "tensor"), whole, whole, whole, whole),
        check_vma=False,
    )
```

```python
import functools

import jax
import jax.numpy as jnp
from jax import lax
from jax.experimental import pallas as pl
from jax.experimental.pallas import tpu as pltpu
from jax.sharding import PartitionSpec as P

MESH = pl.DeviceIdType.MESH
PAD = 128004
MU = 0.9
ETA = 0.7
ALPHA = 0.5
NX = 8
NY = 4
BITS = 5
TOK = 128
DF = 1024
HALF = 512
KV = 256
LAG = 2


def near_first(step):
    return 1 + step // 2 + lax.rem(step, 2) * (6 - 2 * (step // 2))


def each(count, body):
    def step(i, nothing):
        body(i)
        return nothing

    lax.fori_loop(0, count, step, 0)


def contract(left, right, dims):
    return lax.dot_general(left, right, (dims, ((), ())), preferred_element_type=jnp.float32)


def kernel(
    bit,
    frag_ref, ids_hbm, x_hbm, gain_hbm, w_hbm, c_hbm, anchor_hbm, mom_hbm,
    value_ref, back_ref, grad_ref, new_anchor_ref, new_mom_ref, merged_ref,
    ids_ref, x_ref, gain_ref, w_ref, c_ref, anchor_ref, mom_ref,
    c_all, c_four, w_all, xn, xr, acc_ref, fin, vsend, vr, delta, gossip, inv_ref,
    load, c_send, c_recv, cy_send, cy_recv, four_send, four_recv, w_send, w_recv,
    x_send, near_send, near_recv, far_send, far_recv, v_send, v_recv, b_send, b_recv, g_send, g_recv,
):
    r = lax.axis_index("replica")
    f = lax.axis_index("fsdp")
    t = lax.axis_index("tensor")
    h = t // 2
    inward = t + 1 - 2 * h
    outward = t - 1 + 2 * h
    middle = jnp.logical_or(t == 1, t == 2)
    end = jnp.logical_not(middle)

    def column(offset):
        return lax.rem(f + offset + NX, NX)

    partner = r + (1 << bit) * (1 - 2 * lax.rem(r // (1 << bit), 2))

    def push(src, dst, send, recv, **where):
        return pltpu.make_async_remote_copy(
            src_ref=src, dst_ref=dst, send_sem=send, recv_sem=recv, device_id=where, device_id_type=MESH
        )

    w_own = w_all.at[t]
    pairs = (
        (c_hbm, c_ref), (ids_hbm, ids_ref), (w_hbm, w_own), (x_hbm, x_ref), (gain_hbm, gain_ref),
        (anchor_hbm, anchor_ref), (mom_hbm, mom_ref), (w_hbm, w_ref),
    )
    loads = [pltpu.make_async_copy(src, dst, load.at[i]) for i, (src, dst) in enumerate(pairs)]
    for copy in loads:
        copy.start()

    home = f // 2
    side = lax.rem(f, 2)
    stays = jnp.logical_and(t == 1, home == 1)

    barrier = pltpu.get_barrier_semaphore()

    def greet(**where):
        pl.semaphore_signal(barrier, inc=1, device_id=where, device_id_type=MESH)

    greet(tensor=inward)
    for d in range(1, NX):
        greet(fsdp=column(d))
    greet(replica=partner)

    @pl.when(middle)
    def _():
        greet(tensor=outward)
        greet(tensor=3 * (1 - h))

    for j in range(2):
        origin = 2 * t + j
        gap = lax.rem(origin - f + NX, NX)

        @pl.when(jnp.logical_not(jnp.logical_and(gap == 0, t == 1)))
        def _():
            greet(fsdp=origin, tensor=1 + lax.rem(gap, 2))

    loads[0].wait()
    loads[1].wait()
    keep = jnp.where(ids_ref[...] != PAD, 1.0, 0.0).astype(jnp.float32)
    keep = jnp.broadcast_to(keep, (TOK, TOK)).T
    for j in range(KV // TOK):
        cols = slice(j * TOK, (j + 1) * TOK)
        c_all[0, :, cols] = (c_ref[:, cols].astype(jnp.float32) * keep).astype(jnp.bfloat16)
    loads[2].wait()

    pl.semaphore_wait(barrier, NX + 2 + jnp.where(middle, 4, 0) - jnp.where(stays, 1, 0))

    def c_copy(d):
        return push(c_all.at[0], c_all.at[d], c_send.at[d], c_recv.at[d], fsdp=column(d))

    def four_copy(d):
        return push(c_four.at[NY], c_four.at[d // 2], four_send.at[d // 2], four_recv.at[d // 2], fsdp=column(d))

    def near_in(d):
        return push(xr.at[h, d], xr.at[h, d], near_send.at[d], near_recv.at[d], tensor=inward)

    def near_across(d):
        return push(xr.at[h, d], xr.at[h, d], near_send.at[d], far_recv.at[d], tensor=inward)

    def far_out(d):
        return push(xr.at[1 - h, d], xr.at[1 - h, d], far_send.at[d], far_recv.at[d], tensor=outward)

    def x_copy(d):
        return push(xn.at[d], xr.at[h, d], x_send.at[d], near_recv.at[d], fsdp=column(d))

    def v_copy(d):
        return push(vsend.at[d], vr.at[d], v_send.at[d], v_recv.at[d], fsdp=column(-d))

    def back_copy(d):
        return push(fin.at[d // 2], place, b_send.at[d // 2], b_recv.at[side], fsdp=column(-d), tensor=home)

    cy_in = push(c_all.at[0], c_four.at[NY, t], cy_send.at[0], cy_recv.at[t], tensor=inward)
    cy_over = push(c_all.at[0], c_four.at[NY, t], cy_send.at[1], cy_recv.at[t], tensor=2 - h)
    w_in = push(w_own, w_own, w_send.at[0], w_recv.at[t], tensor=inward)
    w_pass = push(w_all.at[outward], w_all.at[outward], w_send.at[1], w_recv.at[outward], tensor=inward)
    g_copy = push(delta, gossip, g_send, g_recv, replica=partner)
    place = back_ref.at[:, pl.ds(pl.multiple_of(side * DF, DF), DF)]

    def norm_scale():
        def squares(i, acc):
            start = pl.multiple_of(i * DF, DF)
            block = x_ref[:, pl.ds(start, DF)].astype(jnp.float32)
            for j in range(DF // 128):
                piece = block[:, j * 128 : (j + 1) * 128]
                acc = acc + piece * piece
            return acc

        loads[3].wait()
        loads[4].wait()
        acc = lax.fori_loop(0, NX, squares, jnp.zeros((TOK, 128), jnp.float32))
        mean = jnp.sum(acc, axis=1, keepdims=True) * (1.0 / (NX * DF))
        inv_ref[...] = jnp.broadcast_to(lax.rsqrt(mean + 1e-05), (TOK, 128))

    def normed(start):
        start = pl.multiple_of(start, HALF)
        block = x_ref[:, pl.ds(start, HALF)].astype(jnp.float32)
        return (block * inv_ref[:, :1] * gain_ref[:, pl.ds(start, HALF)]).astype(jnp.bfloat16)

    def own_tokens():
        for j in range(2):
            xr[j, 0] = normed(f * DF + j * HALF)

    p = frag_ref[0]

    def send_delta():
        loads[5].wait()
        loads[6].wait()
        loads[7].wait()
        delta[...] = (anchor_ref[...] - w_ref[p].astype(jnp.float32)).astype(jnp.bfloat16)
        g_copy.start()

    def values(d):
        weight = w_ref[...].reshape(DF, KV)
        lo = contract(xr[0, d], weight[:HALF], ((1,), (0,)))
        hi = contract(xr[1, d], weight[HALF:], ((1,), (0,)))
        return lo + hi

    def send_values(d):
        vsend[d] = values(d).astype(jnp.bfloat16)
        v_copy(d).start()

    @pl.when(end)
    def _():
        w_in.start()
        cy_in.start()
        cy_over.start()
        norm_scale()

        def spread(step):
            d = near_first(step)
            xn[d] = normed(column(d) * DF + h * HALF)
            x_copy(d).start()

        each(NX - 1, spread)
        each(NX - 1, lambda step: c_copy(near_first(step)).start())
        own_tokens()
        send_delta()

        def onward(step):
            d = near_first(step)
            x_copy(d).wait_recv()
            near_in(d).start()

        each(NX - 1, onward)

        def arrived(step):
            d = near_first(step)
            far_out(d).wait_recv()
            send_values(d)

        each(NX - 1, arrived)
        each(NX - 1, lambda step: c_copy(near_first(step)).wait_recv())

    odd = jnp.where(t == 2, 1, 0)

    def finish(n):
        even_slot = jnp.where(n == 3, 4, jnp.where(n == 2, 6, 2 * n))
        odd_slot = jnp.where(n == 3, 5, jnp.where(n == 2, 3, 1 + 6 * n))
        d = jnp.where(odd == 1, odd_slot, even_slot)

        @pl.when(d != 0)
        def _():
            four_copy(d).wait_recv()
            c_all[d] = c_four[d // 2, t]

        held = jnp.where(d == 0, NY, d // 2)

        def add(block):
            acc_ref[...] += contract(c_four[held, block], w_all[block].reshape(DF, KV), ((1,), (1,)))

        acc_ref[...] = jnp.zeros((TOK, DF), jnp.float32)
        each(NY, add)
        fin[d // 2] = acc_ref[...].astype(jnp.bfloat16)
        here = jnp.logical_and(d == 0, stays)

        @pl.when(here)
        def _():
            pltpu.make_async_copy(fin.at[0], place, b_recv.at[side]).start()

        @pl.when(jnp.logical_not(here))
        def _():
            back_copy(d).start()

    @pl.when(middle)
    def _():
        cy_in.start()
        w_in.start()
        c_four[NY, t] = c_all[0]
        for s in range(1, NY):
            row = lax.rem(t + s, NY)
            push(c_all.at[0], c_four.at[NY, row], cy_send.at[0], cy_recv.at[row], tensor=inward).wait_recv()
        for i in (0, 3, 1, 2):
            mine = 2 * i + odd

            @pl.when(mine != 0)
            def _():
                four_copy(mine).start()

        for i in (0, 3, 1, 2):
            other = 2 * i + 1 - odd

            @pl.when(other != 0)
            def _():
                c_copy(other).start()

        norm_scale()
        own_tokens()
        send_delta()
        push(w_own, w_all.at[outward], w_send.at[0], w_recv.at[outward], tensor=inward).wait_recv()
        w_pass.start()

        def step_of(step):
            @pl.when(step < NX - 1)
            def _():
                d = near_first(step)
                near_in(d).wait_recv()
                near_across(d).start()

            @pl.when(step == 3)
            def _():
                push(w_own, w_all.at[inward], w_send.at[0], w_recv.at[inward], tensor=inward).wait_recv()
                past = 3 * (1 - h)
                push(w_own, w_all.at[past], w_send.at[0], w_recv.at[past], tensor=inward).wait_recv()

            @pl.when(jnp.logical_and(step >= 3, step < NX - 1))
            def _():
                finish(step - 3)

            @pl.when(step >= LAG)
            def _():
                d = near_first(step - LAG)
                far_out(d).wait_recv()
                far_out(d).start()
                send_values(d)

        each(NX - 1 + LAG, step_of)
        for i in range(4):
            mine = 2 * i + odd
            other = 2 * i + 1 - odd

            @pl.when(other != 0)
            def _():
                c_copy(other).wait_recv()
                c_copy(other).wait_send()

            @pl.when(mine != 0)
            def _():
                four_copy(mine).wait_send()

            @pl.when(jnp.logical_not(jnp.logical_and(mine == 0, stays)))
            def _():
                back_copy(mine).wait_send()

    g_copy.wait_recv()
    own_weight = w_ref[p].astype(jnp.float32)
    anchor = anchor_ref[...]
    mean_delta = 0.5 * (anchor - own_weight + gossip[...].astype(jnp.float32))
    momentum = MU * mom_ref[...] + mean_delta
    new_anchor = anchor - ETA * (mean_delta + MU * momentum)
    new_mom_ref[...] = momentum
    new_anchor_ref[...] = new_anchor
    merged_ref[...] = (ALPHA * own_weight + (1.0 - ALPHA) * new_anchor).astype(jnp.bfloat16)

    cotan = c_all[...].reshape(NX * TOK, KV)

    def whole(j):
        block = contract(cotan, xr[j].reshape(NX * TOK, HALF), ((0,), (0,)))
        grad_ref[pl.ds(pl.multiple_of(j * HALF, HALF), HALF), :] = block.T.astype(jnp.bfloat16)

    each(2, whole)
    total = values(0)
    for d in range(1, NX):
        v_copy(d).wait_recv()
        total = total + vr[d].astype(jnp.float32)
    value_ref[...] = total.astype(jnp.bfloat16)

    for j in range(2):
        pltpu.make_async_copy(fin.at[j], back_ref.at[:, j * DF : (j + 1) * DF], b_recv.at[j]).wait()

    w_in.wait_send()
    cy_in.wait_send()
    for d in range(1, NX):
        near_in(d).wait_send()
        v_copy(d).wait_send()
    g_copy.wait_send()

    @pl.when(end)
    def _():
        cy_over.wait_send()
        for d in range(1, NX):
            c_copy(d).wait_send()
            x_copy(d).wait_send()

    @pl.when(middle)
    def _():
        w_pass.wait_send()
        for d in range(1, NX):
            far_out(d).wait_send()


def write_out(*refs):
    n = len(refs) // 2
    copies = [pltpu.make_async_copy(refs[i], refs[n + i], refs[-1].at[i]) for i in range(n)]
    for copy in copies:
        copy.start()
    for copy in copies:
        copy.wait()


def local(
    layer_input, norm_gain, value_weight, value_cotangent, token_ids,
    anchor_weight, outer_momentum, gossip_exponent, fragment_index,
):
    bf16, f32 = jnp.bfloat16, jnp.float32
    smem = pl.BlockSpec(memory_space=pltpu.SMEM)
    vmem = pl.BlockSpec(memory_space=pltpu.VMEM)
    anywhere = pl.BlockSpec(memory_space=pl.ANY)
    dma = pltpu.SemaphoreType.DMA
    frag = anchor_weight.shape[1:]
    shapes = (
        jax.ShapeDtypeStruct((TOK, KV), bf16),
        jax.ShapeDtypeStruct((TOK, 2 * DF), bf16),
        jax.ShapeDtypeStruct((DF, KV), bf16),
        jax.ShapeDtypeStruct(frag, f32),
        jax.ShapeDtypeStruct(frag, f32),
        jax.ShapeDtypeStruct(frag, bf16),
    )
    build = lambda bit: pl.pallas_call(
        functools.partial(kernel, bit),
        out_shape=shapes,
        in_specs=[smem] + [anywhere] * 7,
        out_specs=[vmem] * 6,
        scratch_shapes=[
            pltpu.VMEM((1, TOK), jnp.int32),
            pltpu.VMEM((TOK, NX * DF), bf16),
            pltpu.VMEM((1, NX * DF), f32),
            pltpu.VMEM((4, KV, KV), bf16),
            pltpu.VMEM((TOK, KV), bf16),
            pltpu.VMEM(frag, f32),
            pltpu.VMEM(frag, f32),
            pltpu.VMEM((NX, TOK, KV), bf16),
            pltpu.VMEM((NY + 1, NY, TOK, KV), bf16),
            pltpu.VMEM((NY, 4, KV, KV), bf16),
            pltpu.VMEM((NX, TOK, HALF), bf16),
            pltpu.VMEM((2, NX, TOK, HALF), bf16),
            pltpu.VMEM((TOK, DF), f32),
            pltpu.VMEM((4, TOK, DF), bf16),
            pltpu.VMEM((NX, TOK, KV), bf16),
            pltpu.VMEM((NX, TOK, KV), bf16),
            pltpu.VMEM(frag, bf16),
            pltpu.VMEM(frag, bf16),
            pltpu.VMEM((TOK, 128), f32),
            dma((8,)), dma((NX,)), dma((NX,)), dma((2,)), dma((NY,)), dma((4,)), dma((4,)), dma((2,)), dma((NY,)),
            dma((NX,)), dma((NX,)), dma((NX,)), dma((NX,)), dma((NX,)),
            dma((NX,)), dma((NX,)), dma((4,)), dma((2,)), dma, dma,
        ],
        compiler_params=pltpu.CompilerParams(
            collective_id=bit, has_side_effects=True, vmem_limit_bytes=56 * 1024 * 1024
        ),
        cost_estimate=pl.CostEstimate(flops=2 * 10**9, bytes_accessed=6 * 10**6, transcendentals=128),
    )
    exponent = lax.dynamic_index_in_dim(gossip_exponent, fragment_index[0], 0, keepdims=False)
    outs = lax.switch(
        exponent, [build(bit) for bit in range(BITS)],
        fragment_index, token_ids.reshape(1, TOK), layer_input, norm_gain.reshape(1, NX * DF),
        value_weight.reshape(4, KV, KV), value_cotangent, anchor_weight[0], outer_momentum[0],
    )
    outs = pl.pallas_call(
        write_out,
        out_shape=shapes,
        in_specs=[vmem] * 6,
        out_specs=[anywhere] * 6,
        scratch_shapes=[dma((6,))],
    )(*outs)
    value, back, grad, new_anchor, new_momentum, merged = outs
    return value, back, grad[None], new_anchor[None], new_momentum[None], merged[None]


def solution(mesh):
    tokens = ("replica", "fsdp")
    whole = P("replica", "fsdp", "tensor")
    return jax.shard_map(
        local,
        mesh=mesh,
        in_specs=(P(tokens, None), P(), whole, P(tokens, "tensor"), P(tokens), whole, whole, P(), P()),
        out_specs=(P(tokens, "tensor"), P(tokens, "tensor"), whole, whole, whole, whole),
        check_vma=False,
    )
```
